128 devices in a mesh: slab: 8 (over z, core), space: 16 (over y, x).
Axes of the slice: x: 4, y: 4, z: 4, core: 2. Of those that a mesh axis runs over, the one named last changes fastest.
Arguments:
- frames: bfloat16 [128, 128, 128, 128], P('slab', 'space'), may hold values from -6 to 6
- frame_dest: int32 [128], replicated, may hold values from 0 to 127, as said below
- clip_lengths: int32 [8], replicated, may hold values from 1 to 32, 128 in all
- norm_gain: float32 [128], replicated, may hold values from 0.5 to 1.5
- conv_bias: float32 [128], replicated, may hold values from -3 to 3
- conv_weight: bfloat16 [3, 3, 3, 128, 128], replicated, may hold values from -0.109375 to 0.109375
Outputs:
- encoded: float32 [128, 128, 128, 128], P('slab', None, 'space')
The draws below stay inside these ranges and needn't reach their ends.
Inputs may be any that keep to these rules, and one draw needn't show every extreme that they name: frame_dest is a permutation; for every two slab indices a and b exactly 2 of the frames a * 16 to a * 16 + 15 go to positions b * 16 to b * 16 + 15.
All inputs are finite; a program needn't handle non-finite values.
Results may differ from the reference program's by a relative error of at most 0.0014.
Values may be sent and summed in bfloat16 or wider, within the bound.
A program may use at most 128 MiB of HBM per device.

```python
import math
import jax
import jax.numpy as jnp
import numpy as np
from jax import lax

C = 128
TF = 16
W = 128
NT = 128
H = 128
NCLIP = 8


def draw_frame_dest(key, part):
    slabs = NT // TF
    per_peer = TF // slabs
    dest_keys = jax.random.split(jax.random.fold_in(key, 11), slabs)
    source_keys = jax.random.split(jax.random.fold_in(key, 12), slabs)
    dest_perm = jax.vmap(lambda k: jax.random.permutation(k, TF))(dest_keys)
    source_perm = jax.vmap(lambda k: jax.random.permutation(k, TF))(source_keys)
    source_index = jnp.arange(slabs, dtype=jnp.int32)[:, None]
    target = source_perm // per_peer
    within = source_perm % per_peer
    position = target * TF + dest_perm[target, source_index * per_peer + within]
    return position.reshape(NT).astype(jnp.int32)


def block_levels(key, shape, cuts, least, top_value):
    loudness, own = 1.0, jax.random.fold_in(key, 6)
    for dim, blocks in cuts:
        heights = jnp.exp(jax.random.uniform(jax.random.fold_in(own, dim), (blocks,), jnp.float32, least / len(cuts), top_value / len(cuts)))
        loudness = loudness * jnp.repeat(heights, shape[dim] // blocks).reshape([-1 if axis == dim else 1 for axis in range(len(shape))])
    return loudness


def profile(count, total, reach, skew):
    loads = [(1 << 20) // math.isqrt(standing ** skew) + 1 for standing in range(2, count + 1)]
    rest, counts = total - reach - (count - 1), [1] * (count - 1)
    while rest > 0:
        movable = [i for i in range(count - 1) if counts[i] < reach]
        whole, remaining = sum([loads[i] for i in movable]), rest
        for i in movable:
            more = min(reach - counts[i], max(1, remaining * loads[i] // whole), rest)
            counts[i] = counts[i] + more
            rest = rest - more
    return np.array([reach] + counts)


def uneven_parts(key, amount, total, most, skew):
    if amount == 2:
        one = jax.random.randint(key, (), max(1, total - most), min(most, total - 1) + 1)
        return jnp.stack([one, total - one])
    sizes = jnp.asarray(profile(amount, total, most, skew), jnp.int32)
    pairs = (amount - 1) // 2
    giver, sink = sizes[1:1 + 2 * pairs:2], sizes[2:2 + 2 * pairs:2]
    margin = jnp.minimum(giver - 1, most - sink)
    shifted = jax.random.randint(jax.random.fold_in(key, 1), (pairs,), 0, 1 << 20) % (margin + 1)
    sizes = sizes.at[1:1 + 2 * pairs:2].set(giver - shifted).at[2:2 + 2 * pairs:2].set(sink + shifted)
    return sizes[jax.random.permutation(jax.random.fold_in(key, 2), amount)]


def scatter_about(stream_key, extent, deviation, limit, cuts=(), kind=jnp.bfloat16):
    array = deviation * jax.random.normal(stream_key, extent, jnp.float32)
    if cuts:
        array = array * block_levels(stream_key, extent, cuts, -0.22, 0.18)
    return jnp.clip(array, -limit, limit).astype(kind)


def setup_inputs(seed: int = 0) -> dict:
    keys = jax.random.split(jax.random.key(seed), 7)
    frames = scatter_about(keys[0], (NT, H, W, C), 1.0, 6.0, ((0, 8), (1, 16)))
    frame_dest = draw_frame_dest(jax.random.fold_in(keys[6], 71), 0)
    clip_lengths = uneven_parts(keys[2], NCLIP, NT, 2 * TF, 1).astype(jnp.int32)
    norm_gain = jnp.clip(1.0 + 0.1 * jax.random.normal(keys[3], (C,), jnp.float32), 0.5, 1.5)
    conv_bias = scatter_about(keys[4], (C,), 0.5, 3.0, (), jnp.float32)
    conv_weight = scatter_about(keys[5], (3, 3, 3, C, C), (27 * C) ** -0.5, 0.109375)
    return {"frames": frames, "frame_dest": frame_dest, "clip_lengths": clip_lengths, "norm_gain": norm_gain, "conv_bias": conv_bias, "conv_weight": conv_weight}


def clip_masks(clip_lengths, positions):
    starts = jnp.cumsum(clip_lengths) - clip_lengths
    first_frame = lax.optimization_barrier(jnp.max(jnp.where(starts[None, :] <= positions[:, None], starts[None, :], 0), axis=1))
    lags = jnp.arange(3, dtype=jnp.int32)
    return (positions[:, None] - lags[None, :] >= first_frame[:, None]).astype(jnp.bfloat16)

def normalize(arranged, norm_gain):
    values = arranged.astype(jnp.float32)
    meansq = lax.optimization_barrier(jnp.mean(values * values, axis=-1, keepdims=True))
    return jax.nn.silu(values * lax.rsqrt(meansq + 1e-06) * norm_gain).astype(jnp.bfloat16)

def spatial_conv(inputs, kernel, padding):
    return lax.conv_general_dilated(inputs, kernel, (1, 1), padding, dimension_numbers=('NHWC', 'HWIO', 'NHWC'), preferred_element_type=jnp.float32)

def reference(frames, frame_dest, clip_lengths, norm_gain, conv_bias, conv_weight):
    inverse = jnp.argsort(frame_dest).astype(jnp.int32)
    arranged = jnp.take(frames, inverse, axis=0)
    normed = normalize(arranged, norm_gain)
    masks = clip_masks(clip_lengths, jnp.arange(NT, dtype=jnp.int32))
    branch = jnp.zeros(frames.shape, jnp.float32)
    for frame_lag in range(3):
        moved = jnp.concatenate([jnp.zeros((frame_lag,) + normed.shape[1:], normed.dtype), normed[:NT - frame_lag]], axis=0)
        moved = moved * masks[:, frame_lag][:, None, None, None]
        branch = branch + spatial_conv(moved, conv_weight[frame_lag], ((1, 1), (1, 1)))
    return arranged.astype(jnp.float32) + branch + conv_bias
```

```python
import functools

import jax
import jax.numpy as jnp
from jax import lax
from jax.experimental import pallas as pl
from jax.experimental.pallas import tpu as pltpu
from jax.sharding import PartitionSpec as P

MESH = pl.DeviceIdType.MESH
BF, F32 = jnp.bfloat16, jnp.float32
CH = 128
BAND = 8
PARTS = BAND + 2
AHEAD = 2


def shape_of_space(count):
    side = int(count**0.5)
    return (side, side) if side * side == count else (1, count)


def kernel(
    NS, SY, SX, frames, index, mask, gain, bias, weight, out,
    fr, st, packed, recv, stag, arr, xs, tsend, trecv, wraw, wbig, outv,
    send_sem, recv_sem, tsend_sem, trecv_sem, out_sem, edge_sem, frame_sem, weight_sem,
):
    SP = SY * SX
    TF = 2 * NS
    width = fr.shape[2]
    pairs = 2 if SY > 1 else 1
    groups = SP // pairs
    a = lax.axis_index("slab")
    s = lax.axis_index("space")
    y, x = s // SX, lax.rem(s, SX)

    def loop(count, body, start=0):
        lax.fori_loop(start, count, lambda i, _: (body(i), 0)[1], 0)

    def offset(g, u):
        return g // SX + 2 * u, lax.rem(lax.rem(g, SX) + 2 * u, SX)

    def target(g, u):
        dy, dx = offset(g, u)
        return lax.rem(y + dy, SY) * SX + lax.rem(x + dx, SX)

    def source(g, u):
        dy, dx = offset(g, u)
        return lax.rem(y - dy + SY, SY) * SX + lax.rem(x - dx + SX, SX)

    def group_of(band):
        dy = lax.rem(y - band // SX + SY, SY)
        dx = lax.rem(x - lax.rem(band, SX) + SX, SX)
        u = dy // 2
        return (dy - 2 * u) * SX + lax.rem(dx - 2 * u + 2 * SX, SX)

    def block_copy(c, b, band, slab):
        return pltpu.make_async_remote_copy(
            src_ref=packed.at[c, b], dst_ref=recv.at[band, slab],
            send_sem=send_sem.at[c, b], recv_sem=recv_sem.at[band, slab],
            device_id=(b, c), device_id_type=MESH,
        )

    def tail_copy(band):
        return pltpu.make_async_remote_copy(
            src_ref=tsend.at[band], dst_ref=trecv.at[band],
            send_sem=tsend_sem.at[band], recv_sem=trecv_sem.at[band],
            device_id=(lax.rem(a + 1, NS), s), device_id_type=MESH,
        )

    def frame_copy(i):
        return pltpu.make_async_copy(frames.at[i], fr.at[i], frame_sem.at[i])

    loop(TF, lambda i: frame_copy(i).start())
    weight_copy = pltpu.make_async_copy(weight, wraw, weight_sem)
    weight_copy.start()
    barrier = pltpu.get_barrier_semaphore()

    def greet(i):
        pl.semaphore_signal(
            barrier, inc=1, device_id_type=MESH,
            device_id=(lax.rem(a + i // SP, NS), lax.rem(s + lax.rem(i, SP), SP)),
        )

    loop(NS * SP, greet, 1)
    loop(TF, lambda i: frame_copy(i).wait())

    def pack(b):
        for j in range(2):
            i = index[2 * b + j]
            for h in range(BAND):
                st[j, h * width : (h + 1) * width] = fr[i, h].astype(F32)

        def strip(c):
            for h in range(BAND):
                at = pl.ds(pl.multiple_of(h * width + c * BAND, BAND), BAND)
                packed[c, b, h] = jnp.concatenate([st[0, at], st[1, at]], axis=0).astype(BF)
            for side in range(2):
                if side:
                    column = jnp.minimum(c * BAND + BAND, width - 1)
                    inside = (c < SP - 1).astype(F32)
                else:
                    column = jnp.maximum(c * BAND - 1, 0)
                    inside = (c > 0).astype(F32)
                at = pl.ds(column, BAND, stride=width)
                both = jnp.concatenate([st[0, at], st[1, at]], axis=0)
                packed[c, b, BAND + side] = (both * inside).astype(BF)

        loop(SP, strip)

    loop(NS, pack)
    recv[s, a] = packed[s, a]
    pl.semaphore_wait(barrier, NS * SP - 1)

    def send_group(g):
        count = NS * pairs

        def one(j):
            m = lax.rem(5 * j + 3, count)
            b = lax.rem(a + m // pairs, NS)
            c = target(g, lax.rem(m, pairs))

            @pl.when(jnp.logical_or(b != a, c != s))
            def _():
                block_copy(c, b, s, a).start()

        loop(count, one)

    for g in range(min(AHEAD, groups)):
        send_group(g)

    weight_copy.wait()
    rows = 3 * CH
    for lag in range(3):
        for r in range(4):
            for o in range(2):
                at = (lag, slice(r * rows, (r + 1) * rows), slice(o * CH, (o + 1) * CH))
                if 0 <= r - o <= 2:
                    wbig[at] = wraw[lag, r - o]
                else:
                    wbig[at] = jnp.zeros((rows, CH), BF)
    for r in (0, 1, SP * BAND + 2, SP * BAND + 3):
        xs[r] = jnp.zeros(xs.shape[1:], BF)

    gains = gain[...]
    lines = lax.broadcasted_iota(jnp.int32, (BAND, CH), 0)

    def normalized(v):
        meansq = jnp.mean(v * v, axis=-1, keepdims=True)
        v = v * lax.rsqrt(meansq + 1e-06) * gains
        return 0.5 * v * (1.0 + jnp.tanh(0.5 * v))

    def shifted(body, before, after, h):
        first = jnp.broadcast_to(before[h : h + 1], (BAND, CH))
        last = jnp.broadcast_to(after[h : h + 1], (BAND, CH))
        return (
            jnp.where(lines == 0, first, pltpu.roll(body, 1, 0)),
            body,
            jnp.where(lines == BAND - 1, last, pltpu.roll(body, BAND - 1, 0)),
        )

    def arrive(band):
        def wait_one(k):
            @pl.when(jnp.logical_or(band != s, k != a))
            def _():
                block_copy(s, a, band, k).wait_recv()

        loop(NS, wait_one)

        def stage(k):
            for r in range(PARTS):
                v = recv[band, k, r].astype(F32)
                stag[2 * k, r] = v[:BAND]
                stag[2 * k + 1, r] = v[BAND:]

        loop(NS, stage)
        late, last = index[TF + TF - 2], index[TF + TF - 1]
        for r in range(PARTS):
            both = [normalized(stag[late, r]), normalized(stag[last, r])]
            tsend[band, r] = jnp.concatenate(both, axis=0).astype(BF)
        tail_copy(band).start()

    def spread(band):
        def frame(t):
            parts = []
            for f in range(2):
                slot = index[TF + t + f * NS]
                raw = [stag[slot, r] for r in range(PARTS)]
                parts.append((raw, [normalized(v) for v in raw]))
            for h in range(BAND):
                line = band * BAND + h
                arr[line, t] = jnp.concatenate([parts[0][0][h], parts[1][0][h]], axis=0).astype(BF)
                views = [shifted(n[h], n[BAND], n[BAND + 1], h) for _, n in parts]
                for k in range(3):
                    xs[line + 2, t + 2, :, k * CH : (k + 1) * CH] = jnp.concatenate(
                        [views[0][k], views[1][k]], axis=0
                    ).astype(BF)

        loop(NS, frame)

    def earlier(band):
        tail_copy(band).wait_recv()
        parts = [trecv[band, r].astype(F32) for r in range(PARTS)]
        for q in range(2):
            cut = slice(q * BAND, (q + 1) * BAND)
            for h in range(BAND):
                line = band * BAND + h + 2
                views = shifted(parts[h][cut], parts[BAND][cut], parts[BAND + 1][cut], h)
                for k in range(3):
                    lanes = slice(k * CH, (k + 1) * CH)
                    own = xs[line, NS + q, :, lanes].astype(F32)[:BAND]
                    xs[line, q, :, lanes] = jnp.concatenate([views[k], own], axis=0).astype(BF)

    def conv(starts):
        total = None
        for lag in range(3):
            taps = [
                jnp.concatenate(
                    [xs[r0 + r, 2 - lag : 2 - lag + NS].reshape(NS * 16, rows) for r in range(4)], axis=1
                )
                for r0 in starts
            ]
            taps = taps[0] if len(taps) == 1 else jnp.concatenate(taps, axis=0)
            term = jnp.dot(taps, wbig[lag], preferred_element_type=F32)
            if lag:
                keep = mask[lag - 1].reshape(NS * 16, CH)
                keep = jnp.concatenate([keep, keep], axis=1)
                term = term * (keep if len(starts) == 1 else jnp.concatenate([keep] * len(starts), axis=0))
            total = term if total is None else total + term
        return total

    def put(value, line):
        value = value + bias[...] + arr[line].astype(F32).reshape(NS * 16, CH)
        value = value.reshape(NS, 2, BAND, CH)
        for f in range(2):
            outv[f * NS : (f + 1) * NS, line] = value[:, f]

    def inner_copy(band):
        at = pl.ds(band * BAND + 1, BAND - 2)
        return pltpu.make_async_copy(outv.at[:, at], out.at[:, at], out_sem.at[band])

    def edge_copy(e, lines):
        at = pl.ds(jnp.maximum(e * BAND - 1, 0), lines)
        return pltpu.make_async_copy(outv.at[:, at], out.at[:, at], edge_sem.at[e])

    def inner(band):
        total = conv([band * BAND + 2 + 2 * p for p in range(3)])
        for p in range(3):
            for o in range(2):
                value = total[p * NS * 16 : (p + 1) * NS * 16, o * CH : (o + 1) * CH]
                put(value, band * BAND + 1 + 2 * p + o)
        inner_copy(band).start()

    def edge(e):
        total = conv([e * BAND])

        @pl.when(e > 0)
        def _():
            put(total[:, :CH], e * BAND - 1)

        @pl.when(e < SP)
        def _():
            put(total[:, CH:], e * BAND)

        @pl.when(jnp.logical_and(e > 0, e < SP))
        def _():
            edge_copy(e, 2).start()

        @pl.when(jnp.logical_or(e == 0, e == SP))
        def _():
            edge_copy(e, 1).start()

    def finish(g):
        def each(u):
            band = source(g, u)
            earlier(band)
            inner(band)

        loop(pairs, each)

        def maybe(e):
            low = group_of(jnp.maximum(e - 1, 0))
            high = group_of(jnp.minimum(e, SP - 1))

            @pl.when(jnp.maximum(low, high) == g)
            def _():
                edge(e)

        loop(SP + 1, maybe)

    def step(g):
        @pl.when(g < groups)
        def _():
            def each(u):
                band = source(g, u)
                arrive(band)
                spread(band)

            loop(pairs, each)

            @pl.when(g + AHEAD < groups)
            def _():
                send_group(g + AHEAD)

        @pl.when(g > 0)
        def _():
            finish(g - 1)

    loop(groups + 1, step)

    def drain(i):
        c, b = i // NS, lax.rem(i, NS)

        @pl.when(jnp.logical_or(b != a, c != s))
        def _():
            block_copy(c, b, s, a).wait_send()

    loop(NS * SP, drain)

    def close(band):
        tail_copy(band).wait_send()
        inner_copy(band).wait()

    loop(SP, close)
    edge_copy(0, 1).wait()
    loop(SP, lambda e: edge_copy(e, 2).wait(), 1)
    edge_copy(SP, 1).wait()


def orders(frame_dest, clip_lengths, slabs, per_slab, slab):
    where = frame_dest.reshape(slabs, per_slab)
    slot = jnp.arange(2 * slabs, dtype=jnp.int32)
    lane = jnp.arange(per_slab, dtype=jnp.int32)
    own = lax.dynamic_index_in_dim(where, slab, 0, keepdims=False) // per_slab
    meant = own[None, :] == (slot // 2)[:, None]
    low = jnp.min(jnp.where(meant, lane[None, :], per_slab), axis=1)
    high = jnp.max(jnp.where(meant, lane[None, :], -1), axis=1)
    send = jnp.where(slot % 2 == 0, low, high)
    here = where // per_slab == slab
    first = jnp.min(jnp.where(here, lane[None, :], per_slab), axis=1)
    second = lane[None, :] != first[:, None]
    slots = 2 * jnp.arange(slabs, dtype=jnp.int32)[:, None] + second.astype(jnp.int32)
    position = slab * per_slab + lane
    hit = where[None, :, :] == position[:, None, None]
    pick = jnp.sum(jnp.where(hit, slots[None], 0), axis=(1, 2))
    index = jnp.concatenate([send, pick]).astype(jnp.int32)
    clips = jnp.arange(clip_lengths.shape[0], dtype=jnp.int32)
    starts = jnp.sum(jnp.where(clips[:, None] < clips[None, :], clip_lengths[:, None], 0), axis=0)
    begin = jnp.max(jnp.where(starts[None, :] <= position[:, None], starts[None, :], 0), axis=1)
    lags = jnp.arange(1, 3, dtype=jnp.int32)
    keep = (position[None, :] - lags[:, None] >= begin[None, :]).astype(F32)
    keep = keep.reshape(2, 2, slabs).transpose(0, 2, 1)[:, :, :, None, None]
    keep = jnp.broadcast_to(keep, (2, slabs, 2, BAND, CH)).reshape(2, slabs, 2 * BAND, CH)
    return index, keep


def local(frames, frame_dest, clip_lengths, norm_gain, conv_bias, conv_weight):
    NS, SP = lax.axis_size("slab"), lax.axis_size("space")
    SY, SX = shape_of_space(SP)
    TF, _, width, _ = frames.shape
    lines = SP * BAND
    index, mask = orders(frame_dest, clip_lengths, NS, TF, lax.axis_index("slab"))
    vmem = pl.BlockSpec(memory_space=pltpu.VMEM)
    held = pl.BlockSpec(memory_space=pl.ANY)
    V, D = pltpu.VMEM, pltpu.SemaphoreType.DMA
    blocks = (SP, NS, PARTS, 2 * BAND, CH)
    return pl.pallas_call(
        functools.partial(kernel, NS, SY, SX),
        out_shape=jax.ShapeDtypeStruct((TF, lines, BAND, CH), F32),
        in_specs=[held, pl.BlockSpec(memory_space=pltpu.SMEM), vmem, vmem, vmem, held],
        out_specs=held,
        scratch_shapes=[
            V((TF, BAND, width, CH), BF),
            V((2, BAND * width, CH), F32),
            V(blocks, BF),
            V(blocks, BF),
            V((TF, PARTS, BAND, CH), F32),
            V((lines, NS, 2 * BAND, CH), BF),
            V((lines + 4, NS + 2, 2 * BAND, 3 * CH), BF),
            V((SP, PARTS, 2 * BAND, CH), BF),
            V((SP, PARTS, 2 * BAND, CH), BF),
            V((3, 3, 3 * CH, CH), BF),
            V((3, 12 * CH, 2 * CH), BF),
            V((TF, lines, BAND, CH), F32),
            D((SP, NS)),
            D((SP, NS)),
            D((SP,)),
            D((SP,)),
            D((SP,)),
            D((SP + 1,)),
            D((TF,)),
            D,
        ],
        compiler_params=pltpu.CompilerParams(
            collective_id=0, has_side_effects=True, vmem_limit_bytes=60 * 2**20
        ),
        cost_estimate=pl.CostEstimate(flops=2 * 10**10, bytes_accessed=2 * 10**7, transcendentals=10**7),
    )(
        frames, index, mask, norm_gain.reshape(1, CH), conv_bias.reshape(1, CH),
        conv_weight.reshape(3, 3, 3 * CH, CH),
    )


def solution(mesh):
    placed = (P("slab", "space", None, None), P(), P(), P(), P(), P())
    return jax.shard_map(
        local, mesh=mesh, in_specs=placed, out_specs=P("slab", None, "space", None), check_vma=False
    )
```

```python
import functools

import jax
import jax.numpy as jnp
from jax import lax
from jax.experimental import pallas as pl
from jax.experimental.pallas import tpu as pltpu
from jax.sharding import PartitionSpec as P

MESH = pl.DeviceIdType.MESH
BF, F32 = jnp.bfloat16, jnp.float32
CH = 128
BAND = 8
PARTS = BAND + 2
AHEAD = 2
BEHIND = 1


def shape_of_space(count):
    side = int(count**0.5)
    return (side, side) if side * side == count else (1, count)


def kernel(
    NS, SY, SX, frames, index, mask, gain, bias, weight, outv,
    fr, st, packed, recv, stag, arr, xs, tsend, trecv, wraw, wbig,
    send_sem, recv_sem, tsend_sem, trecv_sem, frame_sem, weight_sem,
):
    SP = SY * SX
    TF = 2 * NS
    width = fr.shape[2]
    pairs = 2 if SY > 1 else 1
    groups = SP // pairs
    a = lax.axis_index("slab")
    s = lax.axis_index("space")
    y, x = s // SX, lax.rem(s, SX)

    def loop(count, body, start=0):
        lax.fori_loop(start, count, lambda i, _: (body(i), 0)[1], 0)

    def offset(g, u):
        return g // SX + 2 * u, lax.rem(lax.rem(g, SX) + 2 * u, SX)

    def target(g, u):
        dy, dx = offset(g, u)
        return lax.rem(y + dy, SY) * SX + lax.rem(x + dx, SX)

    def source(g, u):
        dy, dx = offset(g, u)
        return lax.rem(y - dy + SY, SY) * SX + lax.rem(x - dx + SX, SX)

    def group_of(band):
        dy = lax.rem(y - band // SX + SY, SY)
        dx = lax.rem(x - lax.rem(band, SX) + SX, SX)
        u = dy // 2
        return (dy - 2 * u) * SX + lax.rem(dx - 2 * u + 2 * SX, SX)

    def block_copy(c, b, band, slab):
        return pltpu.make_async_remote_copy(
            src_ref=packed.at[c, b], dst_ref=recv.at[band, slab],
            send_sem=send_sem.at[c, b], recv_sem=recv_sem.at[band, slab],
            device_id=(b, c), device_id_type=MESH,
        )

    def tail_copy(band):
        return pltpu.make_async_remote_copy(
            src_ref=tsend.at[band], dst_ref=trecv.at[band],
            send_sem=tsend_sem.at[band], recv_sem=trecv_sem.at[band],
            device_id=(lax.rem(a + 1, NS), s), device_id_type=MESH,
        )

    def frame_copy(i):
        return pltpu.make_async_copy(frames.at[i], fr.at[i], frame_sem.at[i])

    loop(TF, lambda i: frame_copy(i).start())
    weight_copy = pltpu.make_async_copy(weight, wraw, weight_sem)
    weight_copy.start()
    barrier = pltpu.get_barrier_semaphore()

    def greet(i):
        pl.semaphore_signal(
            barrier, inc=1, device_id_type=MESH,
            device_id=(lax.rem(a + i // SP, NS), lax.rem(s + lax.rem(i, SP), SP)),
        )

    loop(NS * SP, greet, 1)
    loop(TF, lambda i: frame_copy(i).wait())

    def pack(b):
        for j in range(2):
            i = index[2 * b + j]
            for h in range(BAND):
                st[j, h * width : (h + 1) * width] = fr[i, h].astype(F32)

        def strip(c):
            for h in range(BAND):
                at = pl.ds(pl.multiple_of(h * width + c * BAND, BAND), BAND)
                packed[c, b, h] = jnp.concatenate([st[0, at], st[1, at]], axis=0).astype(BF)
            for side in range(2):
                if side:
                    column = jnp.minimum(c * BAND + BAND, width - 1)
                    inside = (c < SP - 1).astype(F32)
                else:
                    column = jnp.maximum(c * BAND - 1, 0)
                    inside = (c > 0).astype(F32)
                at = pl.ds(column, BAND, stride=width)
                both = jnp.concatenate([st[0, at], st[1, at]], axis=0)
                packed[c, b, BAND + side] = (both * inside).astype(BF)

        loop(SP, strip)

    loop(NS, pack)
    recv[s, a] = packed[s, a]
    pl.semaphore_wait(barrier, NS * SP - 1)

    def send_group(g):
        count = NS * pairs

        def one(j):
            m = lax.rem(5 * j + 3, count)
            b = lax.rem(a + m // pairs, NS)
            c = target(g, lax.rem(m, pairs))

            @pl.when(jnp.logical_or(b != a, c != s))
            def _():
                block_copy(c, b, s, a).start()

        loop(count, one)

    for g in range(min(AHEAD, groups)):
        send_group(g)

    weight_copy.wait()
    rows = 3 * CH
    for lag in range(3):
        for r in range(4):
            for o in range(2):
                at = (lag, slice(r * rows, (r + 1) * rows), slice(o * CH, (o + 1) * CH))
                if 0 <= r - o <= 2:
                    wbig[at] = wraw[lag, r - o]
                else:
                    wbig[at] = jnp.zeros((rows, CH), BF)
    for r in (0, 1, SP * BAND + 2, SP * BAND + 3):
        xs[r] = jnp.zeros(xs.shape[1:], BF)

    gains = gain[...]
    lines = lax.broadcasted_iota(jnp.int32, (BAND, CH), 0)

    def normalized(v):
        meansq = jnp.mean(v * v, axis=-1, keepdims=True)
        v = v * lax.rsqrt(meansq + 1e-06) * gains
        return 0.5 * v * (1.0 + jnp.tanh(0.5 * v))

    def shifted(body, before, after, h):
        first = jnp.broadcast_to(before[h : h + 1], (BAND, CH))
        last = jnp.broadcast_to(after[h : h + 1], (BAND, CH))
        return (
            jnp.where(lines == 0, first, pltpu.roll(body, 1, 0)),
            body,
            jnp.where(lines == BAND - 1, last, pltpu.roll(body, BAND - 1, 0)),
        )

    def wait_blocks(band):
        def wait_one(k):
            @pl.when(jnp.logical_or(band != s, k != a))
            def _():
                block_copy(s, a, band, k).wait_recv()

        loop(NS, wait_one)

    def arrive(band):
        def stage(k):
            for r in range(PARTS):
                v = recv[band, k, r].astype(F32)
                stag[2 * k, r] = v[:BAND]
                stag[2 * k + 1, r] = v[BAND:]

        loop(NS, stage)
        late, last = index[TF + TF - 2], index[TF + TF - 1]
        for r in range(PARTS):
            both = [normalized(stag[late, r]), normalized(stag[last, r])]
            tsend[band, r] = jnp.concatenate(both, axis=0).astype(BF)
        tail_copy(band).start()

    def spread(band):
        def frame(t):
            parts = []
            for f in range(2):
                slot = index[TF + t + f * NS]
                raw = [stag[slot, r] for r in range(PARTS)]
                parts.append((raw, [normalized(v) for v in raw]))
            for h in range(BAND):
                line = band * BAND + h
                arr[line, t] = jnp.concatenate([parts[0][0][h], parts[1][0][h]], axis=0).astype(BF)
                views = [shifted(n[h], n[BAND], n[BAND + 1], h) for _, n in parts]
                for k in range(3):
                    xs[line + 2, t + 2, :, k * CH : (k + 1) * CH] = jnp.concatenate(
                        [views[0][k], views[1][k]], axis=0
                    ).astype(BF)

        loop(NS, frame)

    def earlier(band):
        tail_copy(band).wait_recv()
        parts = [trecv[band, r].astype(F32) for r in range(PARTS)]
        for q in range(2):
            cut = slice(q * BAND, (q + 1) * BAND)
            for h in range(BAND):
                line = band * BAND + h + 2
                views = shifted(parts[h][cut], parts[BAND][cut], parts[BAND + 1][cut], h)
                for k in range(3):
                    lanes = slice(k * CH, (k + 1) * CH)
                    own = xs[line, NS + q, :, lanes].astype(F32)[:BAND]
                    xs[line, q, :, lanes] = jnp.concatenate([views[k], own], axis=0).astype(BF)

    def conv(starts):
        total = None
        for lag in range(3):
            taps = [
                jnp.concatenate(
                    [xs[r0 + r, 2 - lag : 2 - lag + NS].reshape(NS * 16, rows) for r in range(4)], axis=1
                )
                for r0 in starts
            ]
            taps = taps[0] if len(taps) == 1 else jnp.concatenate(taps, axis=0)
            term = jnp.dot(taps, wbig[lag], preferred_element_type=F32)
            if lag:
                keep = mask[lag - 1].reshape(NS * 16, CH)
                keep = jnp.concatenate([keep, keep], axis=1)
                term = term * (keep if len(starts) == 1 else jnp.concatenate([keep] * len(starts), axis=0))
            total = term if total is None else total + term
        return total

    def put(value, line):
        value = value + bias[...] + arr[line].astype(F32).reshape(NS * 16, CH)
        value = value.reshape(NS, 2, BAND, CH)
        for f in range(2):
            outv[f * NS : (f + 1) * NS, line] = value[:, f]

    def inner(band):
        total = conv([band * BAND + 2 + 2 * p for p in range(3)])
        for p in range(3):
            for o in range(2):
                value = total[p * NS * 16 : (p + 1) * NS * 16, o * CH : (o + 1) * CH]
                put(value, band * BAND + 1 + 2 * p + o)

    def edge(e):
        total = conv([e * BAND])

        @pl.when(e > 0)
        def _():
            put(total[:, :CH], e * BAND - 1)

        @pl.when(e < SP)
        def _():
            put(total[:, CH:], e * BAND)

    def finish(g):
        def each(u):
            band = source(g, u)
            earlier(band)
            inner(band)

        loop(pairs, each)

        def maybe(e):
            low = group_of(jnp.maximum(e - 1, 0))
            high = group_of(jnp.minimum(e, SP - 1))

            @pl.when(jnp.maximum(low, high) == g)
            def _():
                edge(e)

        loop(SP + 1, maybe)

    def step(g):
        @pl.when(g < groups)
        def _():
            def first(u):
                wait_blocks(source(g, u))

            loop(pairs, first)

            @pl.when(g + AHEAD < groups)
            def _():
                send_group(g + AHEAD)

            def each(u):
                band = source(g, u)
                arrive(band)
                spread(band)

            loop(pairs, each)

        @pl.when(g >= BEHIND)
        def _():
            finish(g - BEHIND)

    loop(groups + BEHIND, step)

    def drain(i):
        c, b = i // NS, lax.rem(i, NS)

        @pl.when(jnp.logical_or(b != a, c != s))
        def _():
            block_copy(c, b, s, a).wait_send()

    loop(NS * SP, drain)

    def close(band):
        tail_copy(band).wait_send()

    loop(SP, close)


def orders(frame_dest, clip_lengths, slabs, per_slab, slab):
    where = frame_dest.reshape(slabs, per_slab)
    slot = jnp.arange(2 * slabs, dtype=jnp.int32)
    lane = jnp.arange(per_slab, dtype=jnp.int32)
    own = lax.dynamic_index_in_dim(where, slab, 0, keepdims=False) // per_slab
    meant = own[None, :] == (slot // 2)[:, None]
    low = jnp.min(jnp.where(meant, lane[None, :], per_slab), axis=1)
    high = jnp.max(jnp.where(meant, lane[None, :], -1), axis=1)
    send = jnp.where(slot % 2 == 0, low, high)
    here = where // per_slab == slab
    first = jnp.min(jnp.where(here, lane[None, :], per_slab), axis=1)
    second = lane[None, :] != first[:, None]
    slots = 2 * jnp.arange(slabs, dtype=jnp.int32)[:, None] + second.astype(jnp.int32)
    position = slab * per_slab + lane
    hit = where[None, :, :] == position[:, None, None]
    pick = jnp.sum(jnp.where(hit, slots[None], 0), axis=(1, 2))
    index = jnp.concatenate([send, pick]).astype(jnp.int32)
    clips = jnp.arange(clip_lengths.shape[0], dtype=jnp.int32)
    starts = jnp.sum(jnp.where(clips[:, None] < clips[None, :], clip_lengths[:, None], 0), axis=0)
    begin = jnp.max(jnp.where(starts[None, :] <= position[:, None], starts[None, :], 0), axis=1)
    lags = jnp.arange(1, 3, dtype=jnp.int32)
    keep = (position[None, :] - lags[:, None] >= begin[None, :]).astype(F32)
    keep = keep.reshape(2, 2, slabs).transpose(0, 2, 1)[:, :, :, None, None]
    keep = jnp.broadcast_to(keep, (2, slabs, 2, BAND, CH)).reshape(2, slabs, 2 * BAND, CH)
    return index, keep


def local(frames, frame_dest, clip_lengths, norm_gain, conv_bias, conv_weight):
    NS, SP = lax.axis_size("slab"), lax.axis_size("space")
    SY, SX = shape_of_space(SP)
    TF, _, width, _ = frames.shape
    lines = SP * BAND
    index, mask = orders(frame_dest, clip_lengths, NS, TF, lax.axis_index("slab"))
    vmem = pl.BlockSpec(memory_space=pltpu.VMEM)
    held = pl.BlockSpec(memory_space=pl.ANY)
    V, D = pltpu.VMEM, pltpu.SemaphoreType.DMA
    blocks = (SP, NS, PARTS, 2 * BAND, CH)
    return pl.pallas_call(
        functools.partial(kernel, NS, SY, SX),
        out_shape=pltpu.VMEM((TF, lines, BAND, CH), F32),
        in_specs=[held, pl.BlockSpec(memory_space=pltpu.SMEM), vmem, vmem, vmem, held],
        out_specs=vmem,
        scratch_shapes=[
            V((TF, BAND, width, CH), BF),
            V((2, BAND * width, CH), F32),
            V(blocks, BF),
            V(blocks, BF),
            V((TF, PARTS, BAND, CH), F32),
            V((lines, NS, 2 * BAND, CH), BF),
            V((lines + 4, NS + 2, 2 * BAND, 3 * CH), BF),
            V((SP, PARTS, 2 * BAND, CH), BF),
            V((SP, PARTS, 2 * BAND, CH), BF),
            V((3, 3, 3 * CH, CH), BF),
            V((3, 12 * CH, 2 * CH), BF),
            D((SP, NS)),
            D((SP, NS)),
            D((SP,)),
            D((SP,)),
            D((TF,)),
            D,
        ],
        compiler_params=pltpu.CompilerParams(
            collective_id=0, has_side_effects=True, vmem_limit_bytes=46 * 2**20
        ),
        cost_estimate=pl.CostEstimate(flops=2 * 10**10, bytes_accessed=2 * 10**7, transcendentals=10**7),
    )(
        frames, index, mask, norm_gain.reshape(1, CH), conv_bias.reshape(1, CH),
        conv_weight.reshape(3, 3, 3 * CH, CH),
    )


def solution(mesh):
    placed = (P("slab", "space", None, None), P(), P(), P(), P(), P())
    return jax.shard_map(
        local, mesh=mesh, in_specs=placed, out_specs=P("slab", None, "space", None), check_vma=False
    )
```

```python
import functools

import jax
import jax.numpy as jnp
from jax import lax
from jax.experimental import pallas as pl
from jax.experimental.pallas import tpu as pltpu
from jax.sharding import PartitionSpec as P

MESH = pl.DeviceIdType.MESH
BF, F32 = jnp.bfloat16, jnp.float32
CH = 128
BAND = 8
PARTS = BAND + 2
AHEAD = 2
BEHIND = 1


def shape_of_space(count):
    side = int(count**0.5)
    return (side, side) if side * side == count else (1, count)


def kernel(
    NS, SY, SX, frames, index, mask, gain, bias, weight, outv,
    fr, st, packed, recv, stag, arr, xs, tsend, trecv, wraw, wbig,
    send_sem, recv_sem, tsend_sem, trecv_sem, frame_sem, weight_sem,
):
    SP = SY * SX
    TF = 2 * NS
    width = fr.shape[2]
    pairs = 2 if SY > 1 else 1
    groups = SP // pairs
    a = lax.axis_index("slab")
    s = lax.axis_index("space")
    y, x = s // SX, lax.rem(s, SX)

    def loop(count, body, start=0):
        lax.fori_loop(start, count, lambda i, _: (body(i), 0)[1], 0)

    def offset(g, u):
        return g // SX + 2 * u, lax.rem(lax.rem(g, SX) + 2 * u, SX)

    def target(g, u):
        dy, dx = offset(g, u)
        return lax.rem(y + dy, SY) * SX + lax.rem(x + dx, SX)

    def source(g, u):
        dy, dx = offset(g, u)
        return lax.rem(y - dy + SY, SY) * SX + lax.rem(x - dx + SX, SX)

    def group_of(band):
        dy = lax.rem(y - band // SX + SY, SY)
        dx = lax.rem(x - lax.rem(band, SX) + SX, SX)
        u = dy // 2
        return (dy - 2 * u) * SX + lax.rem(dx - 2 * u + 2 * SX, SX)

    def block_copy(c, b, band, slab):
        return pltpu.make_async_remote_copy(
            src_ref=packed.at[c, b], dst_ref=recv.at[band, slab],
            send_sem=send_sem.at[c, b], recv_sem=recv_sem.at[band, slab],
            device_id=(b, c), device_id_type=MESH,
        )

    def tail_copy(band):
        return pltpu.make_async_remote_copy(
            src_ref=tsend.at[band], dst_ref=trecv.at[band],
            send_sem=tsend_sem.at[band], recv_sem=trecv_sem.at[band],
            device_id=(lax.rem(a + 1, NS), s), device_id_type=MESH,
        )

    def frame_copy(i):
        return pltpu.make_async_copy(frames.at[i], fr.at[i], frame_sem.at[i])

    loop(TF, lambda i: frame_copy(i).start())
    weight_copy = pltpu.make_async_copy(weight, wraw, weight_sem)
    weight_copy.start()
    barrier = pltpu.get_barrier_semaphore()

    def greet(i):
        pl.semaphore_signal(
            barrier, inc=1, device_id_type=MESH,
            device_id=(lax.rem(a + i // SP, NS), lax.rem(s + lax.rem(i, SP), SP)),
        )

    loop(NS * SP, greet, 1)
    loop(TF, lambda i: frame_copy(i).wait())

    def pack(b):
        for j in range(2):
            i = index[2 * b + j]
            for h in range(BAND):
                st[j, h * width : (h + 1) * width] = fr[i, h].astype(F32)

        def strip(c):
            for h in range(BAND):
                at = pl.ds(pl.multiple_of(h * width + c * BAND, BAND), BAND)
                packed[c, b, h] = jnp.concatenate([st[0, at], st[1, at]], axis=0).astype(BF)
            for side in range(2):
                if side:
                    column = jnp.minimum(c * BAND + BAND, width - 1)
                    inside = (c < SP - 1).astype(F32)
                else:
                    column = jnp.maximum(c * BAND - 1, 0)
                    inside = (c > 0).astype(F32)
                at = pl.ds(column, BAND, stride=width)
                both = jnp.concatenate([st[0, at], st[1, at]], axis=0)
                packed[c, b, BAND + side] = (both * inside).astype(BF)

        loop(SP, strip)

    loop(NS, pack)
    recv[s, a] = packed[s, a]
    pl.semaphore_wait(barrier, NS * SP - 1)

    def send_group(g):
        count = NS * pairs

        def one(j):
            m = lax.rem(5 * j + 3, count)
            b = lax.rem(a + m // pairs, NS)
            c = target(g, lax.rem(m, pairs))

            @pl.when(jnp.logical_or(b != a, c != s))
            def _():
                block_copy(c, b, s, a).start()

        loop(count, one)

    for g in range(min(AHEAD, groups)):
        send_group(g)

    weight_copy.wait()
    rows = 3 * CH
    for lag in range(3):
        for r in range(4):
            for o in range(2):
                at = (lag, slice(r * rows, (r + 1) * rows), slice(o * CH, (o + 1) * CH))
                if 0 <= r - o <= 2:
                    wbig[at] = wraw[lag, r - o]
                else:
                    wbig[at] = jnp.zeros((rows, CH), BF)
    for r in (0, 1, SP * BAND + 2, SP * BAND + 3):
        xs[r] = jnp.zeros(xs.shape[1:], BF)

    gains = gain[...]
    lines = lax.broadcasted_iota(jnp.int32, (BAND, CH), 0)

    def normalized(v):
        meansq = jnp.mean(v * v, axis=-1, keepdims=True)
        v = v * lax.rsqrt(meansq + 1e-06) * gains
        return 0.5 * v * (1.0 + jnp.tanh(0.5 * v))

    def shifted(body, before, after, h):
        first = jnp.broadcast_to(before[h : h + 1], (BAND, CH))
        last = jnp.broadcast_to(after[h : h + 1], (BAND, CH))
        return (
            jnp.where(lines == 0, first, pltpu.roll(body, 1, 0)),
            body,
            jnp.where(lines == BAND - 1, last, pltpu.roll(body, BAND - 1, 0)),
        )

    def wait_blocks(band):
        def wait_one(k):
            @pl.when(jnp.logical_or(band != s, k != a))
            def _():
                block_copy(s, a, band, k).wait_recv()

        loop(NS, wait_one)

    def arrive(band):
        def stage(k):
            for r in range(PARTS):
                v = recv[band, k, r].astype(F32)
                stag[2 * k, r] = v[:BAND]
                stag[2 * k + 1, r] = v[BAND:]

        loop(NS, stage)
        late, last = index[TF + TF - 2], index[TF + TF - 1]
        for r in range(PARTS):
            both = [normalized(stag[late, r]), normalized(stag[last, r])]
            tsend[band, r] = jnp.concatenate(both, axis=0).astype(BF)
        tail_copy(band).start()

    def spread(band):
        def frame(t):
            parts = []
            for f in range(2):
                slot = index[TF + t + f * NS]
                raw = [stag[slot, r] for r in range(PARTS)]
                parts.append((raw, [normalized(v) for v in raw]))
            for h in range(BAND):
                line = band * BAND + h
                arr[line, t] = jnp.concatenate([parts[0][0][h], parts[1][0][h]], axis=0).astype(BF)
                views = [shifted(n[h], n[BAND], n[BAND + 1], h) for _, n in parts]
                for k in range(3):
                    xs[line + 2, t + 2, :, k * CH : (k + 1) * CH] = jnp.concatenate(
                        [views[0][k], views[1][k]], axis=0
                    ).astype(BF)

        lax.fori_loop(0, NS, lambda i, _: (frame(i), 0)[1], 0, unroll=2)

    def earlier(band):
        tail_copy(band).wait_recv()
        parts = [trecv[band, r].astype(F32) for r in range(PARTS)]
        for q in range(2):
            cut = slice(q * BAND, (q + 1) * BAND)
            for h in range(BAND):
                line = band * BAND + h + 2
                views = shifted(parts[h][cut], parts[BAND][cut], parts[BAND + 1][cut], h)
                for k in range(3):
                    lanes = slice(k * CH, (k + 1) * CH)
                    own = xs[line, NS + q, :, lanes].astype(F32)[:BAND]
                    xs[line, q, :, lanes] = jnp.concatenate([views[k], own], axis=0).astype(BF)

    def conv(starts):
        total = None
        for lag in range(3):
            taps = [
                jnp.concatenate(
                    [xs[r0 + r, 2 - lag : 2 - lag + NS].reshape(NS * 16, rows) for r in range(4)], axis=1
                )
                for r0 in starts
            ]
            taps = taps[0] if len(taps) == 1 else jnp.concatenate(taps, axis=0)
            term = jnp.dot(taps, wbig[lag], preferred_element_type=F32)
            if lag:
                keep = mask[lag - 1].reshape(NS * 16, CH)
                keep = jnp.concatenate([keep, keep], axis=1)
                term = term * (keep if len(starts) == 1 else jnp.concatenate([keep] * len(starts), axis=0))
            total = term if total is None else total + term
        return total

    def put(value, line):
        value = value + bias[...] + arr[line].astype(F32).reshape(NS * 16, CH)
        value = value.reshape(NS, 2, BAND, CH)
        for f in range(2):
            outv[f * NS : (f + 1) * NS, line] = value[:, f]

    def inner(band):
        total = conv([band * BAND + 2 + 2 * p for p in range(3)])
        for p in range(3):
            for o in range(2):
                value = total[p * NS * 16 : (p + 1) * NS * 16, o * CH : (o + 1) * CH]
                put(value, band * BAND + 1 + 2 * p + o)

    def edge(e):
        total = conv([e * BAND])

        @pl.when(e > 0)
        def _():
            put(total[:, :CH], e * BAND - 1)

        @pl.when(e < SP)
        def _():
            put(total[:, CH:], e * BAND)

    def finish(g):
        def each(u):
            band = source(g, u)
            earlier(band)
            inner(band)

        loop(pairs, each)

        def maybe(e):
            low = group_of(jnp.maximum(e - 1, 0))
            high = group_of(jnp.minimum(e, SP - 1))

            @pl.when(jnp.maximum(low, high) == g)
            def _():
                edge(e)

        loop(SP + 1, maybe)

    def step(g):
        @pl.when(g < groups)
        def _():
            def first(u):
                wait_blocks(source(g, u))

            loop(pairs, first)

            @pl.when(g + AHEAD < groups)
            def _():
                send_group(g + AHEAD)

            def each(u):
                band = source(g, u)
                arrive(band)
                spread(band)

            loop(pairs, each)

        @pl.when(g >= BEHIND)
        def _():
            finish(g - BEHIND)

    loop(groups + BEHIND, step)

    def drain(i):
        c, b = i // NS, lax.rem(i, NS)

        @pl.when(jnp.logical_or(b != a, c != s))
        def _():
            block_copy(c, b, s, a).wait_send()

    loop(NS * SP, drain)

    def close(band):
        tail_copy(band).wait_send()

    loop(SP, close)


def orders(frame_dest, clip_lengths, slabs, per_slab, slab):
    where = frame_dest.reshape(slabs, per_slab)
    slot = jnp.arange(2 * slabs, dtype=jnp.int32)
    lane = jnp.arange(per_slab, dtype=jnp.int32)
    own = lax.dynamic_index_in_dim(where, slab, 0, keepdims=False) // per_slab
    meant = own[None, :] == (slot // 2)[:, None]
    low = jnp.min(jnp.where(meant, lane[None, :], per_slab), axis=1)
    high = jnp.max(jnp.where(meant, lane[None, :], -1), axis=1)
    send = jnp.where(slot % 2 == 0, low, high)
    here = where // per_slab == slab
    first = jnp.min(jnp.where(here, lane[None, :], per_slab), axis=1)
    second = lane[None, :] != first[:, None]
    slots = 2 * jnp.arange(slabs, dtype=jnp.int32)[:, None] + second.astype(jnp.int32)
    position = slab * per_slab + lane
    hit = where[None, :, :] == position[:, None, None]
    pick = jnp.sum(jnp.where(hit, slots[None], 0), axis=(1, 2))
    index = jnp.concatenate([send, pick]).astype(jnp.int32)
    clips = jnp.arange(clip_lengths.shape[0], dtype=jnp.int32)
    starts = jnp.sum(jnp.where(clips[:, None] < clips[None, :], clip_lengths[:, None], 0), axis=0)
    begin = jnp.max(jnp.where(starts[None, :] <= position[:, None], starts[None, :], 0), axis=1)
    lags = jnp.arange(1, 3, dtype=jnp.int32)
    keep = (position[None, :] - lags[:, None] >= begin[None, :]).astype(F32)
    keep = keep.reshape(2, 2, slabs).transpose(0, 2, 1)[:, :, :, None, None]
    keep = jnp.broadcast_to(keep, (2, slabs, 2, BAND, CH)).reshape(2, slabs, 2 * BAND, CH)
    return index, keep


def local(frames, frame_dest, clip_lengths, norm_gain, conv_bias, conv_weight):
    NS, SP = lax.axis_size("slab"), lax.axis_size("space")
    SY, SX = shape_of_space(SP)
    TF, _, width, _ = frames.shape
    lines = SP * BAND
    index, mask = orders(frame_dest, clip_lengths, NS, TF, lax.axis_index("slab"))
    vmem = pl.BlockSpec(memory_space=pltpu.VMEM)
    held = pl.BlockSpec(memory_space=pl.ANY)
    V, D = pltpu.VMEM, pltpu.SemaphoreType.DMA
    blocks = (SP, NS, PARTS, 2 * BAND, CH)
    return pl.pallas_call(
        functools.partial(kernel, NS, SY, SX),
        out_shape=pltpu.VMEM((TF, lines, BAND, CH), F32),
        in_specs=[held, pl.BlockSpec(memory_space=pltpu.SMEM), vmem, vmem, vmem, held],
        out_specs=vmem,
        scratch_shapes=[
            V((TF, BAND, width, CH), BF),
            V((2, BAND * width, CH), F32),
            V(blocks, BF),
            V(blocks, BF),
            V((TF, PARTS, BAND, CH), F32),
            V((lines, NS, 2 * BAND, CH), BF),
            V((lines + 4, NS + 2, 2 * BAND, 3 * CH), BF),
            V((SP, PARTS, 2 * BAND, CH), BF),
            V((SP, PARTS, 2 * BAND, CH), BF),
            V((3, 3, 3 * CH, CH), BF),
            V((3, 12 * CH, 2 * CH), BF),
            D((SP, NS)),
            D((SP, NS)),
            D((SP,)),
            D((SP,)),
            D((TF,)),
            D,
        ],
        compiler_params=pltpu.CompilerParams(
            collective_id=0, has_side_effects=True, vmem_limit_bytes=46 * 2**20
        ),
        cost_estimate=pl.CostEstimate(flops=2 * 10**10, bytes_accessed=2 * 10**7, transcendentals=10**7),
    )(
        frames, index, mask, norm_gain.reshape(1, CH), conv_bias.reshape(1, CH),
        conv_weight.reshape(3, 3, 3 * CH, CH),
    )


def solution(mesh):
    placed = (P("slab", "space", None, None), P(), P(), P(), P(), P())
    return jax.shard_map(
        local, mesh=mesh, in_specs=placed, out_specs=P("slab", None, "space", None), check_vma=False
    )
```

```python
import functools

import jax
import jax.numpy as jnp
from jax import lax
from jax.experimental import pallas as pl
from jax.experimental.pallas import tpu as pltpu
from jax.sharding import PartitionSpec as P

MESH = pl.DeviceIdType.MESH
BF, F32 = jnp.bfloat16, jnp.float32
CH = 128
BAND = 8
PARTS = BAND + 2
AHEAD = 2
BEHIND = 1


def shape_of_space(count):
    side = int(count**0.5)
    return (side, side) if side * side == count else (1, count)


def kernel(
    NS, SY, SX, frames, index, mask, gain, bias, weight, outv,
    fr, st, packed, recv, stag, arr, xs, tsend, trecv, wraw, wbig,
    send_sem, recv_sem, tsend_sem, trecv_sem, frame_sem, weight_sem,
):
    SP = SY * SX
    TF = 2 * NS
    width = fr.shape[2]
    pairs = 2 if SY > 1 else 1
    groups = SP // pairs
    a = lax.axis_index("slab")
    s = lax.axis_index("space")
    y, x = s // SX, lax.rem(s, SX)

    def loop(count, body, start=0):
        lax.fori_loop(start, count, lambda i, _: (body(i), 0)[1], 0)

    def offset(g, u):
        return g // SX + 2 * u, lax.rem(lax.rem(g, SX) + 2 * u, SX)

    def target(g, u):
        dy, dx = offset(g, u)
        return lax.rem(y + dy, SY) * SX + lax.rem(x + dx, SX)

    def source(g, u):
        dy, dx = offset(g, u)
        return lax.rem(y - dy + SY, SY) * SX + lax.rem(x - dx + SX, SX)

    def group_of(band):
        dy = lax.rem(y - band // SX + SY, SY)
        dx = lax.rem(x - lax.rem(band, SX) + SX, SX)
        u = dy // 2
        return (dy - 2 * u) * SX + lax.rem(dx - 2 * u + 2 * SX, SX)

    def block_copy(c, b, band, slab):
        return pltpu.make_async_remote_copy(
            src_ref=packed.at[c, b], dst_ref=recv.at[band, slab],
            send_sem=send_sem.at[c, b], recv_sem=recv_sem.at[band, slab],
            device_id=(b, c), device_id_type=MESH,
        )

    def tail_copy(band):
        return pltpu.make_async_remote_copy(
            src_ref=tsend.at[band], dst_ref=trecv.at[band],
            send_sem=tsend_sem.at[band], recv_sem=trecv_sem.at[band],
            device_id=(lax.rem(a + 1, NS), s), device_id_type=MESH,
        )

    def frame_copy(i):
        return pltpu.make_async_copy(frames.at[i], fr.at[i], frame_sem.at[i])

    loop(TF, lambda i: frame_copy(i).start())
    weight_copy = pltpu.make_async_copy(weight, wraw, weight_sem)
    weight_copy.start()
    barrier = pltpu.get_barrier_semaphore()

    def greet(i):
        pl.semaphore_signal(
            barrier, inc=1, device_id_type=MESH,
            device_id=(lax.rem(a + i // SP, NS), lax.rem(s + lax.rem(i, SP), SP)),
        )

    loop(NS * SP, greet, 1)
    loop(TF, lambda i: frame_copy(i).wait())

    def pack(b):
        for j in range(2):
            i = index[2 * b + j]
            for h in range(BAND):
                st[j, h * width : (h + 1) * width] = fr[i, h].astype(F32)

        def strip(c):
            for h in range(BAND):
                at = pl.ds(pl.multiple_of(h * width + c * BAND, BAND), BAND)
                packed[c, b, h] = jnp.concatenate([st[0, at], st[1, at]], axis=0).astype(BF)
            for side in range(2):
                if side:
                    column = jnp.minimum(c * BAND + BAND, width - 1)
                    inside = (c < SP - 1).astype(F32)
                else:
                    column = jnp.maximum(c * BAND - 1, 0)
                    inside = (c > 0).astype(F32)
                at = pl.ds(column, BAND, stride=width)
                both = jnp.concatenate([st[0, at], st[1, at]], axis=0)
                packed[c, b, BAND + side] = (both * inside).astype(BF)

        loop(SP, strip)

    loop(NS, pack)
    recv[s, a] = packed[s, a]
    pl.semaphore_wait(barrier, NS * SP - 1)

    def send_group(g):
        count = NS * pairs

        def one(j):
            m = lax.rem(5 * j + 3, count)
            b = lax.rem(a + m // pairs, NS)
            c = target(g, lax.rem(m, pairs))

            @pl.when(jnp.logical_or(b != a, c != s))
            def _():
                block_copy(c, b, s, a).start()

        loop(count, one)

    for g in range(min(AHEAD, groups)):
        send_group(g)

    weight_copy.wait()
    rows = 3 * CH
    for lag in range(3):
        for r in range(4):
            for o in range(2):
                at = (lag, slice(r * rows, (r + 1) * rows), slice(o * CH, (o + 1) * CH))
                if 0 <= r - o <= 2:
                    wbig[at] = wraw[lag, r - o]
                else:
                    wbig[at] = jnp.zeros((rows, CH), BF)
    for r in (0, 1, SP * BAND + 2, SP * BAND + 3):
        xs[r] = jnp.zeros(xs.shape[1:], BF)

    gains = gain[...]
    lines = lax.broadcasted_iota(jnp.int32, (BAND, CH), 0)

    def normalized(v):
        meansq = jnp.mean(v * v, axis=-1, keepdims=True)
        v = v * lax.rsqrt(meansq + 1e-06) * gains
        return 0.5 * v * (1.0 + jnp.tanh(0.5 * v))

    def shifted(body, before, after, h):
        first = jnp.broadcast_to(before[h : h + 1], (BAND, CH))
        last = jnp.broadcast_to(after[h : h + 1], (BAND, CH))
        return (
            jnp.where(lines == 0, first, pltpu.roll(body, 1, 0)),
            body,
            jnp.where(lines == BAND - 1, last, pltpu.roll(body, BAND - 1, 0)),
        )

    def wait_blocks(band):
        def wait_one(k):
            @pl.when(jnp.logical_or(band != s, k != a))
            def _():
                block_copy(s, a, band, k).wait_recv()

        loop(NS, wait_one)

    def arrive(band):
        def stage(k):
            for r in range(PARTS):
                v = recv[band, k, r].astype(F32)
                stag[2 * k, r] = v[:BAND]
                stag[2 * k + 1, r] = v[BAND:]

        lax.fori_loop(0, NS, lambda i, _: (stage(i), 0)[1], 0, unroll=2)
        late, last = index[TF + TF - 2], index[TF + TF - 1]
        for r in range(PARTS):
            both = [normalized(stag[late, r]), normalized(stag[last, r])]
            tsend[band, r] = jnp.concatenate(both, axis=0).astype(BF)
        tail_copy(band).start()

    def spread(band):
        def frame(t):
            parts = []
            for f in range(2):
                slot = index[TF + t + f * NS]
                raw = [stag[slot, r] for r in range(PARTS)]
                parts.append((raw, [normalized(v) for v in raw]))
            for h in range(BAND):
                line = band * BAND + h
                arr[line, t] = jnp.concatenate([parts[0][0][h], parts[1][0][h]], axis=0).astype(BF)
                views = [shifted(n[h], n[BAND], n[BAND + 1], h) for _, n in parts]
                for k in range(3):
                    xs[line + 2, t + 2, :, k * CH : (k + 1) * CH] = jnp.concatenate(
                        [views[0][k], views[1][k]], axis=0
                    ).astype(BF)

        lax.fori_loop(0, NS, lambda i, _: (frame(i), 0)[1], 0, unroll=2)

    def earlier(band):
        tail_copy(band).wait_recv()
        parts = [trecv[band, r].astype(F32) for r in range(PARTS)]
        for q in range(2):
            cut = slice(q * BAND, (q + 1) * BAND)
            for h in range(BAND):
                line = band * BAND + h + 2
                views = shifted(parts[h][cut], parts[BAND][cut], parts[BAND + 1][cut], h)
                for k in range(3):
                    lanes = slice(k * CH, (k + 1) * CH)
                    own = xs[line, NS + q, :, lanes].astype(F32)[:BAND]
                    xs[line, q, :, lanes] = jnp.concatenate([views[k], own], axis=0).astype(BF)

    def conv(starts):
        total = None
        for lag in range(3):
            taps = [
                jnp.concatenate(
                    [xs[r0 + r, 2 - lag : 2 - lag + NS].reshape(NS * 16, rows) for r in range(4)], axis=1
                )
                for r0 in starts
            ]
            taps = taps[0] if len(taps) == 1 else jnp.concatenate(taps, axis=0)
            term = jnp.dot(taps, wbig[lag], preferred_element_type=F32)
            if lag:
                keep = mask[lag - 1].reshape(NS * 16, CH)
                keep = jnp.concatenate([keep, keep], axis=1)
                term = term * (keep if len(starts) == 1 else jnp.concatenate([keep] * len(starts), axis=0))
            total = term if total is None else total + term
        return total

    def put(value, line):
        value = value + bias[...] + arr[line].astype(F32).reshape(NS * 16, CH)
        value = value.reshape(NS, 2, BAND, CH)
        for f in range(2):
            outv[f * NS : (f + 1) * NS, line] = value[:, f]

    def inner(band):
        total = conv([band * BAND + 2 + 2 * p for p in range(3)])
        for p in range(3):
            for o in range(2):
                value = total[p * NS * 16 : (p + 1) * NS * 16, o * CH : (o + 1) * CH]
                put(value, band * BAND + 1 + 2 * p + o)

    def edge(e):
        total = conv([e * BAND])

        @pl.when(e > 0)
        def _():
            put(total[:, :CH], e * BAND - 1)

        @pl.when(e < SP)
        def _():
            put(total[:, CH:], e * BAND)

    def finish(g):
        def each(u):
            band = source(g, u)
            earlier(band)
            inner(band)

        loop(pairs, each)

        def maybe(e):
            low = group_of(jnp.maximum(e - 1, 0))
            high = group_of(jnp.minimum(e, SP - 1))

            @pl.when(jnp.maximum(low, high) == g)
            def _():
                edge(e)

        loop(SP + 1, maybe)

    def step(g):
        @pl.when(g < groups)
        def _():
            def first(u):
                wait_blocks(source(g, u))

            loop(pairs, first)

            @pl.when(g + AHEAD < groups)
            def _():
                send_group(g + AHEAD)

            def each(u):
                band = source(g, u)
                arrive(band)
                spread(band)

            loop(pairs, each)

        @pl.when(g >= BEHIND)
        def _():
            finish(g - BEHIND)

    loop(groups + BEHIND, step)

    def drain(i):
        c, b = i // NS, lax.rem(i, NS)

        @pl.when(jnp.logical_or(b != a, c != s))
        def _():
            block_copy(c, b, s, a).wait_send()

    loop(NS * SP, drain)

    def close(band):
        tail_copy(band).wait_send()

    loop(SP, close)


def orders(frame_dest, clip_lengths, slabs, per_slab, slab):
    where = frame_dest.reshape(slabs, per_slab)
    slot = jnp.arange(2 * slabs, dtype=jnp.int32)
    lane = jnp.arange(per_slab, dtype=jnp.int32)
    own = lax.dynamic_index_in_dim(where, slab, 0, keepdims=False) // per_slab
    meant = own[None, :] == (slot // 2)[:, None]
    low = jnp.min(jnp.where(meant, lane[None, :], per_slab), axis=1)
    high = jnp.max(jnp.where(meant, lane[None, :], -1), axis=1)
    send = jnp.where(slot % 2 == 0, low, high)
    here = where // per_slab == slab
    first = jnp.min(jnp.where(here, lane[None, :], per_slab), axis=1)
    second = lane[None, :] != first[:, None]
    slots = 2 * jnp.arange(slabs, dtype=jnp.int32)[:, None] + second.astype(jnp.int32)
    position = slab * per_slab + lane
    hit = where[None, :, :] == position[:, None, None]
    pick = jnp.sum(jnp.where(hit, slots[None], 0), axis=(1, 2))
    index = jnp.concatenate([send, pick]).astype(jnp.int32)
    clips = jnp.arange(clip_lengths.shape[0], dtype=jnp.int32)
    starts = jnp.sum(jnp.where(clips[:, None] < clips[None, :], clip_lengths[:, None], 0), axis=0)
    begin = jnp.max(jnp.where(starts[None, :] <= position[:, None], starts[None, :], 0), axis=1)
    lags = jnp.arange(1, 3, dtype=jnp.int32)
    keep = (position[None, :] - lags[:, None] >= begin[None, :]).astype(F32)
    keep = keep.reshape(2, 2, slabs).transpose(0, 2, 1)[:, :, :, None, None]
    keep = jnp.broadcast_to(keep, (2, slabs, 2, BAND, CH)).reshape(2, slabs, 2 * BAND, CH)
    return index, keep


def local(frames, frame_dest, clip_lengths, norm_gain, conv_bias, conv_weight):
    NS, SP = lax.axis_size("slab"), lax.axis_size("space")
    SY, SX = shape_of_space(SP)
    TF, _, width, _ = frames.shape
    lines = SP * BAND
    index, mask = orders(frame_dest, clip_lengths, NS, TF, lax.axis_index("slab"))
    vmem = pl.BlockSpec(memory_space=pltpu.VMEM)
    held = pl.BlockSpec(memory_space=pl.ANY)
    V, D = pltpu.VMEM, pltpu.SemaphoreType.DMA
    blocks = (SP, NS, PARTS, 2 * BAND, CH)
    return pl.pallas_call(
        functools.partial(kernel, NS, SY, SX),
        out_shape=pltpu.VMEM((TF, lines, BAND, CH), F32),
        in_specs=[held, pl.BlockSpec(memory_space=pltpu.SMEM), vmem, vmem, vmem, held],
        out_specs=vmem,
        scratch_shapes=[
            V((TF, BAND, width, CH), BF),
            V((2, BAND * width, CH), F32),
            V(blocks, BF),
            V(blocks, BF),
            V((TF, PARTS, BAND, CH), F32),
            V((lines, NS, 2 * BAND, CH), BF),
            V((lines + 4, NS + 2, 2 * BAND, 3 * CH), BF),
            V((SP, PARTS, 2 * BAND, CH), BF),
            V((SP, PARTS, 2 * BAND, CH), BF),
            V((3, 3, 3 * CH, CH), BF),
            V((3, 12 * CH, 2 * CH), BF),
            D((SP, NS)),
            D((SP, NS)),
            D((SP,)),
            D((SP,)),
            D((TF,)),
            D,
        ],
        compiler_params=pltpu.CompilerParams(
            collective_id=0, has_side_effects=True, vmem_limit_bytes=46 * 2**20
        ),
        cost_estimate=pl.CostEstimate(flops=2 * 10**10, bytes_accessed=2 * 10**7, transcendentals=10**7),
    )(
        frames, index, mask, norm_gain.reshape(1, CH), conv_bias.reshape(1, CH),
        conv_weight.reshape(3, 3, 3 * CH, CH),
    )


def solution(mesh):
    placed = (P("slab", "space", None, None), P(), P(), P(), P(), P())
    return jax.shard_map(
        local, mesh=mesh, in_specs=placed, out_specs=P("slab", None, "space", None), check_vma=False
    )
```

```python
import functools

import jax
import jax.numpy as jnp
from jax import lax
from jax.experimental import pallas as pl
from jax.experimental.pallas import tpu as pltpu
from jax.sharding import PartitionSpec as P

MESH = pl.DeviceIdType.MESH
BF, F32 = jnp.bfloat16, jnp.float32
CH = 128
BAND = 8
PARTS = BAND + 2
AHEAD = 2
BEHIND = 1


def shape_of_space(count):
    side = int(count**0.5)
    return (side, side) if side * side == count else (1, count)


def kernel(
    NS, SY, SX, frames, index, mask, gain, bias, weight, outv,
    fr, st, packed, recv, stag, arr, xs, tsend, trecv, wraw, wbig,
    send_sem, recv_sem, tsend_sem, trecv_sem, frame_sem, weight_sem,
):
    SP = SY * SX
    TF = 2 * NS
    width = fr.shape[2]
    pairs = 2 if SY > 1 else 1
    groups = SP // pairs
    a = lax.axis_index("slab")
    s = lax.axis_index("space")
    y, x = s // SX, lax.rem(s, SX)

    def loop(count, body, start=0):
        lax.fori_loop(start, count, lambda i, _: (body(i), 0)[1], 0)

    def offset(g, u):
        return g // SX + 2 * u, lax.rem(lax.rem(g, SX) + 2 * u, SX)

    def target(g, u):
        dy, dx = offset(g, u)
        return lax.rem(y + dy, SY) * SX + lax.rem(x + dx, SX)

    def source(g, u):
        dy, dx = offset(g, u)
        return lax.rem(y - dy + SY, SY) * SX + lax.rem(x - dx + SX, SX)

    def group_of(band):
        dy = lax.rem(y - band // SX + SY, SY)
        dx = lax.rem(x - lax.rem(band, SX) + SX, SX)
        u = dy // 2
        return (dy - 2 * u) * SX + lax.rem(dx - 2 * u + 2 * SX, SX)

    def block_copy(c, b, band, slab):
        return pltpu.make_async_remote_copy(
            src_ref=packed.at[c, b], dst_ref=recv.at[band, slab],
            send_sem=send_sem.at[c, b], recv_sem=recv_sem.at[band, slab],
            device_id=(b, c), device_id_type=MESH,
        )

    def tail_copy(band):
        return pltpu.make_async_remote_copy(
            src_ref=tsend.at[band], dst_ref=trecv.at[band],
            send_sem=tsend_sem.at[band], recv_sem=trecv_sem.at[band],
            device_id=(lax.rem(a + 1, NS), s), device_id_type=MESH,
        )

    def frame_copy(i):
        return pltpu.make_async_copy(frames.at[i], fr.at[i], frame_sem.at[i])

    loop(TF, lambda i: frame_copy(i).start())
    weight_copy = pltpu.make_async_copy(weight, wraw, weight_sem)
    weight_copy.start()
    barrier = pltpu.get_barrier_semaphore()

    def greet(i):
        pl.semaphore_signal(
            barrier, inc=1, device_id_type=MESH,
            device_id=(lax.rem(a + i // SP, NS), lax.rem(s + lax.rem(i, SP), SP)),
        )

    loop(NS * SP, greet, 1)
    loop(TF, lambda i: frame_copy(i).wait())

    def pack(b):
        for j in range(2):
            i = index[2 * b + j]
            for h in range(BAND):
                st[j, h * width : (h + 1) * width] = fr[i, h].astype(F32)

        def strip(c):
            for h in range(BAND):
                at = pl.ds(pl.multiple_of(h * width + c * BAND, BAND), BAND)
                packed[c, b, h] = jnp.concatenate([st[0, at], st[1, at]], axis=0).astype(BF)
            for side in range(2):
                if side:
                    column = jnp.minimum(c * BAND + BAND, width - 1)
                    inside = (c < SP - 1).astype(F32)
                else:
                    column = jnp.maximum(c * BAND - 1, 0)
                    inside = (c > 0).astype(F32)
                at = pl.ds(column, BAND, stride=width)
                both = jnp.concatenate([st[0, at], st[1, at]], axis=0)
                packed[c, b, BAND + side] = (both * inside).astype(BF)

        loop(SP, strip)

    loop(NS, pack)
    recv[s, a] = packed[s, a]
    pl.semaphore_wait(barrier, NS * SP - 1)

    def drain_group(g):
        def one(j):
            b, c = j // pairs, target(g, lax.rem(j, pairs))

            @pl.when(jnp.logical_or(b != a, c != s))
            def _():
                block_copy(c, b, s, a).wait_send()

        loop(NS * pairs, one)

    def send_group(g):
        count = NS * pairs

        def one(j):
            m = lax.rem(5 * j + 3, count)
            b = lax.rem(a + m // pairs, NS)
            c = target(g, lax.rem(m, pairs))

            @pl.when(jnp.logical_or(b != a, c != s))
            def _():
                block_copy(c, b, s, a).start()

        loop(count, one)

    for g in range(min(AHEAD, groups)):
        send_group(g)

    weight_copy.wait()
    rows = 3 * CH
    for lag in range(3):
        for r in range(4):
            for o in range(2):
                at = (lag, slice(r * rows, (r + 1) * rows), slice(o * CH, (o + 1) * CH))
                if 0 <= r - o <= 2:
                    wbig[at] = wraw[lag, r - o]
                else:
                    wbig[at] = jnp.zeros((rows, CH), BF)
    for r in (0, 1, SP * BAND + 2, SP * BAND + 3):
        xs[r] = jnp.zeros(xs.shape[1:], BF)

    gains = gain[...]
    lines = lax.broadcasted_iota(jnp.int32, (BAND, CH), 0)

    def normalized(v):
        meansq = jnp.mean(v * v, axis=-1, keepdims=True)
        v = v * lax.rsqrt(meansq + 1e-06) * gains
        return 0.5 * v * (1.0 + jnp.tanh(0.5 * v))

    def shifted(body, before, after, h):
        first = jnp.broadcast_to(before[h : h + 1], (BAND, CH))
        last = jnp.broadcast_to(after[h : h + 1], (BAND, CH))
        return (
            jnp.where(lines == 0, first, pltpu.roll(body, 1, 0)),
            body,
            jnp.where(lines == BAND - 1, last, pltpu.roll(body, BAND - 1, 0)),
        )

    def wait_blocks(band):
        def wait_one(k):
            @pl.when(jnp.logical_or(band != s, k != a))
            def _():
                block_copy(s, a, band, k).wait_recv()

        loop(NS, wait_one)

    def arrive(band):
        def stage(k):
            for r in range(PARTS):
                v = recv[band, k, r].astype(F32)
                stag[2 * k, r] = v[:BAND]
                stag[2 * k + 1, r] = v[BAND:]

        loop(NS, stage)
        late, last = index[TF + TF - 2], index[TF + TF - 1]
        for r in range(PARTS):
            both = [normalized(stag[late, r]), normalized(stag[last, r])]
            tsend[band, r] = jnp.concatenate(both, axis=0).astype(BF)
        tail_copy(band).start()

    def spread(band):
        def frame(t):
            parts = []
            for f in range(2):
                slot = index[TF + t + f * NS]
                raw = [stag[slot, r] for r in range(PARTS)]
                parts.append((raw, [normalized(v) for v in raw]))
            for h in range(BAND):
                line = band * BAND + h
                arr[line, t] = jnp.concatenate([parts[0][0][h], parts[1][0][h]], axis=0).astype(BF)
                views = [shifted(n[h], n[BAND], n[BAND + 1], h) for _, n in parts]
                for k in range(3):
                    xs[line + 2, t + 2, :, k * CH : (k + 1) * CH] = jnp.concatenate(
                        [views[0][k], views[1][k]], axis=0
                    ).astype(BF)

        lax.fori_loop(0, NS, lambda i, _: (frame(i), 0)[1], 0, unroll=2)

    def earlier(band):
        tail_copy(band).wait_recv()
        parts = [trecv[band, r].astype(F32) for r in range(PARTS)]
        for q in range(2):
            cut = slice(q * BAND, (q + 1) * BAND)
            for h in range(BAND):
                line = band * BAND + h + 2
                views = shifted(parts[h][cut], parts[BAND][cut], parts[BAND + 1][cut], h)
                for k in range(3):
                    lanes = slice(k * CH, (k + 1) * CH)
                    own = xs[line, NS + q, :, lanes].astype(F32)[:BAND]
                    xs[line, q, :, lanes] = jnp.concatenate([views[k], own], axis=0).astype(BF)

    def conv(starts):
        total = None
        for lag in range(3):
            taps = [
                jnp.concatenate(
                    [xs[r0 + r, 2 - lag : 2 - lag + NS].reshape(NS * 16, rows) for r in range(4)], axis=1
                )
                for r0 in starts
            ]
            taps = taps[0] if len(taps) == 1 else jnp.concatenate(taps, axis=0)
            term = jnp.dot(taps, wbig[lag], preferred_element_type=F32)
            if lag:
                keep = mask[lag - 1].reshape(NS * 16, CH)
                keep = jnp.concatenate([keep, keep], axis=1)
                term = term * (keep if len(starts) == 1 else jnp.concatenate([keep] * len(starts), axis=0))
            total = term if total is None else total + term
        return total

    def put(value, line):
        value = value + bias[...] + arr[line].astype(F32).reshape(NS * 16, CH)
        value = value.reshape(NS, 2, BAND, CH)
        for f in range(2):
            outv[f * NS : (f + 1) * NS, line] = value[:, f]

    def inner(band):
        total = conv([band * BAND + 2 + 2 * p for p in range(3)])
        for p in range(3):
            for o in range(2):
                value = total[p * NS * 16 : (p + 1) * NS * 16, o * CH : (o + 1) * CH]
                put(value, band * BAND + 1 + 2 * p + o)

    def edge(e):
        total = conv([e * BAND])

        @pl.when(e > 0)
        def _():
            put(total[:, :CH], e * BAND - 1)

        @pl.when(e < SP)
        def _():
            put(total[:, CH:], e * BAND)

    def finish(g):
        def each(u):
            band = source(g, u)
            earlier(band)
            inner(band)

        loop(pairs, each)

        def maybe(e):
            low = group_of(jnp.maximum(e - 1, 0))
            high = group_of(jnp.minimum(e, SP - 1))

            @pl.when(jnp.maximum(low, high) == g)
            def _():
                edge(e)

        loop(SP + 1, maybe)

    def step(g):
        @pl.when(g < groups)
        def _():
            def first(u):
                wait_blocks(source(g, u))

            loop(pairs, first)

            @pl.when(g + AHEAD < groups)
            def _():
                send_group(g + AHEAD)

            def each(u):
                band = source(g, u)
                arrive(band)
                spread(band)

            loop(pairs, each)

        @pl.when(jnp.logical_and(g >= 2, g < groups))
        def _():
            drain_group(g - 2)

        @pl.when(g >= BEHIND)
        def _():
            finish(g - BEHIND)

    loop(groups + BEHIND, step)

    for g in range(max(groups - 2, 0), groups):
        drain_group(g)

    def close(band):
        tail_copy(band).wait_send()

    loop(SP, close)


def orders(frame_dest, clip_lengths, slabs, per_slab, slab):
    where = frame_dest.reshape(slabs, per_slab)
    slot = jnp.arange(2 * slabs, dtype=jnp.int32)
    lane = jnp.arange(per_slab, dtype=jnp.int32)
    own = lax.dynamic_index_in_dim(where, slab, 0, keepdims=False) // per_slab
    meant = own[None, :] == (slot // 2)[:, None]
    low = jnp.min(jnp.where(meant, lane[None, :], per_slab), axis=1)
    high = jnp.max(jnp.where(meant, lane[None, :], -1), axis=1)
    send = jnp.where(slot % 2 == 0, low, high)
    here = where // per_slab == slab
    first = jnp.min(jnp.where(here, lane[None, :], per_slab), axis=1)
    second = lane[None, :] != first[:, None]
    slots = 2 * jnp.arange(slabs, dtype=jnp.int32)[:, None] + second.astype(jnp.int32)
    position = slab * per_slab + lane
    hit = where[None, :, :] == position[:, None, None]
    pick = jnp.sum(jnp.where(hit, slots[None], 0), axis=(1, 2))
    index = jnp.concatenate([send, pick]).astype(jnp.int32)
    clips = jnp.arange(clip_lengths.shape[0], dtype=jnp.int32)
    starts = jnp.sum(jnp.where(clips[:, None] < clips[None, :], clip_lengths[:, None], 0), axis=0)
    begin = jnp.max(jnp.where(starts[None, :] <= position[:, None], starts[None, :], 0), axis=1)
    lags = jnp.arange(1, 3, dtype=jnp.int32)
    keep = (position[None, :] - lags[:, None] >= begin[None, :]).astype(F32)
    keep = keep.reshape(2, 2, slabs).transpose(0, 2, 1)[:, :, :, None, None]
    keep = jnp.broadcast_to(keep, (2, slabs, 2, BAND, CH)).reshape(2, slabs, 2 * BAND, CH)
    return index, keep


def local(frames, frame_dest, clip_lengths, norm_gain, conv_bias, conv_weight):
    NS, SP = lax.axis_size("slab"), lax.axis_size("space")
    SY, SX = shape_of_space(SP)
    TF, _, width, _ = frames.shape
    lines = SP * BAND
    index, mask = orders(frame_dest, clip_lengths, NS, TF, lax.axis_index("slab"))
    vmem = pl.BlockSpec(memory_space=pltpu.VMEM)
    held = pl.BlockSpec(memory_space=pl.ANY)
    V, D = pltpu.VMEM, pltpu.SemaphoreType.DMA
    blocks = (SP, NS, PARTS, 2 * BAND, CH)
    return pl.pallas_call(
        functools.partial(kernel, NS, SY, SX),
        out_shape=pltpu.VMEM((TF, lines, BAND, CH), F32),
        in_specs=[held, pl.BlockSpec(memory_space=pltpu.SMEM), vmem, vmem, vmem, held],
        out_specs=vmem,
        scratch_shapes=[
            V((TF, BAND, width, CH), BF),
            V((2, BAND * width, CH), F32),
            V(blocks, BF),
            V(blocks, BF),
            V((TF, PARTS, BAND, CH), F32),
            V((lines, NS, 2 * BAND, CH), BF),
            V((lines + 4, NS + 2, 2 * BAND, 3 * CH), BF),
            V((SP, PARTS, 2 * BAND, CH), BF),
            V((SP, PARTS, 2 * BAND, CH), BF),
            V((3, 3, 3 * CH, CH), BF),
            V((3, 12 * CH, 2 * CH), BF),
            D((SP, NS)),
            D((SP, NS)),
            D((SP,)),
            D((SP,)),
            D((TF,)),
            D,
        ],
        compiler_params=pltpu.CompilerParams(
            collective_id=0, has_side_effects=True, vmem_limit_bytes=46 * 2**20
        ),
        cost_estimate=pl.CostEstimate(flops=2 * 10**10, bytes_accessed=2 * 10**7, transcendentals=10**7),
    )(
        frames, index, mask, norm_gain.reshape(1, CH), conv_bias.reshape(1, CH),
        conv_weight.reshape(3, 3, 3 * CH, CH),
    )


def solution(mesh):
    placed = (P("slab", "space", None, None), P(), P(), P(), P(), P())
    return jax.shard_map(
        local, mesh=mesh, in_specs=placed, out_specs=P("slab", None, "space", None), check_vma=False
    )
```
